32 devices in a mesh: groups: 2 (over x), op: 16 (over z, y, core).
Axes of the slice: x: 2, y: 2, z: 4, core: 2. Of those that a mesh axis runs over, the one named last changes fastest.
Arguments:
- wavefunction: bfloat16 [256, 3, 128, 128], P(('groups', 'op')), parts along dimension 0, as said below
- left_env: bfloat16 [64, 128, 128, 128], P(('groups', 'op')), parts along dimension 0, as said below
- right_env: bfloat16 [64, 128, 128, 128], P(('groups', 'op')), parts along dimension 0, as said below
- term_shift: int32 [64], P('groups'), parts along dimension 0, may hold values from 0 to 2
- sector_width: int32 [256], P(('groups', 'op')), parts along dimension 0, may hold values from 1 to 128, as said below
Outputs:
- sigma_out: float32 [256, 3, 128, 128], P(('groups', 'op')), parts along dimension 0
The draws below stay inside these ranges and needn't reach their ends.
There are 2 independent parts, one for each index of `groups`. The reference program is written for one: setup_inputs(seed, part) draws one part's arguments, and reference() takes and returns one part's arrays. A program takes and returns all parts, laid end to end along the dimension named above; each array names one. Nothing has to cross between parts.
Inputs may be any that keep to these rules, and one draw needn't show every extreme that they name: `sector_width`: sector widths sum to 12288 and exactly one sector has width 128. `wavefunction`: rows and columns at or past a sector's width are zero in that sector's blocks. `left_env`: rows at or past a sector's width are zero in that sector's blocks. `right_env`: rows at or past a sector's width are zero in that sector's blocks.
All inputs are finite; a program needn't handle non-finite values.
Results may differ from the reference program's by a relative error of at most 0.0029.
Values may be sent and summed in bfloat16 or wider, within the bound.
A program may use at most 192 MiB of HBM per device.

```python
import jax
import jax.numpy as jnp
from jax import lax

B = 128
NSEC = 128
TERMS = 32
V = 3
SPLIT = 1
SLOTS = 32
HS = 128
N_OP = 16


def sector_widths(key):
    key = jax.random.fold_in(key, 977)
    key_big, key_order, key_mixed, key_moves = jax.random.split(key, 4)
    whole_sum = NSEC * B * 3 // 4
    remainder = whole_sum - B
    base_width = remainder // (NSEC - 1)
    surplus = remainder - base_width * (NSEC - 1)
    spread = max(0, min(base_width - 1, B - base_width - 2))
    pair_count = (NSEC - 1) // 2
    ranking = jax.random.permutation(key_order, NSEC - 1)
    surplus_bits = (ranking < surplus).astype(jnp.int32)
    mixing = jax.random.permutation(key_mixed, NSEC - 1)
    steps_drawn = jax.random.randint(key_moves, (pair_count,), -spread, spread + 1, dtype=jnp.int32)
    changes = jnp.zeros((NSEC - 1,), jnp.int32).at[mixing[:pair_count]].add(steps_drawn)
    changes = changes.at[mixing[pair_count:2 * pair_count]].add(-steps_drawn)
    values = base_width + surplus_bits + changes
    where_big = jax.random.randint(key_big, (), 0, NSEC, dtype=jnp.int32)
    places = jnp.arange(NSEC, dtype=jnp.int32)
    before = jnp.take(values, jnp.clip(places, 0, NSEC - 2))
    after = jnp.take(values, jnp.clip(places - 1, 0, NSEC - 2))
    return jnp.where(places < where_big, before, jnp.where(places == where_big, B, after)).astype(jnp.int32)


def env_masked(values, widths):
    sector_of = jnp.arange(HS, dtype=jnp.int32)[None, :] * SPLIT + (jnp.arange(SLOTS, dtype=jnp.int32) // TERMS)[:, None]
    live_width = jnp.take(widths, sector_of)[:, :, None, None]
    line_index = jnp.arange(B, dtype=jnp.int32)
    keep_mask = line_index[None, None, :, None] < live_width
    return jnp.where(keep_mask, values, 0.0).astype(jnp.bfloat16)


def draw_sector_width(key, part):
    return sector_widths(key)


def draw_wavefunction(key, part):
    widths = sector_widths(key)
    key = jax.random.fold_in(key, 3)
    block_shape = (NSEC, V, B, B)
    values = jnp.clip(jax.random.normal(key, block_shape, jnp.float32), -6.0, 6.0)
    line_index = jnp.arange(B, dtype=jnp.int32)
    live_width = widths[:, None, None, None]
    keep_mask = (line_index[None, None, :, None] < live_width) & (line_index[None, None, None, :] < live_width)
    return jnp.where(keep_mask, values, 0.0).astype(jnp.bfloat16)


def draw_left_env(key, part):
    widths = sector_widths(key)
    key = jax.random.fold_in(key, 5)
    block_shape = (SLOTS, HS, B, B)
    scale = B ** (-0.5)
    values = jnp.clip(jax.random.normal(key, block_shape, jnp.float32), -6.0, 6.0) * scale
    return env_masked(values, widths)


def draw_right_env(key, part):
    widths = sector_widths(key)
    key = jax.random.fold_in(key, 7)
    block_shape = (SLOTS, HS, B, B)
    scale = (B * TERMS) ** (-0.5)
    values = jnp.clip(jax.random.normal(key, block_shape, jnp.float32), -6.0, 6.0) * scale
    return env_masked(values, widths)


def place_ends(array, rng, least, largest):
    longest = array.shape.index(max(array.shape))
    spots = []
    for shift in (0, 1):
        where = [jax.random.randint(jax.random.fold_in(rng, axis), (), 0, length) for axis, length in enumerate(array.shape)]
        where[longest] = (where[longest] + shift) % array.shape[longest]
        spots.append(tuple(where))
    return array.at[spots[0]].set(least).at[spots[1]].set(largest)


def setup_inputs(seed: int = 0, part: int = 0) -> dict:
    streams_of = jax.random.split(jax.random.key(seed), 6)
    part_keys = jax.random.split(jax.random.fold_in(streams_of[5], part), 6)
    wavefunction = draw_wavefunction(jax.random.fold_in(jax.random.fold_in(streams_of[5], part), 71), part)
    left_env = draw_left_env(jax.random.fold_in(jax.random.fold_in(streams_of[5], part), 71), part)
    right_env = draw_right_env(jax.random.fold_in(jax.random.fold_in(streams_of[5], part), 71), part)
    term_shift = place_ends(jax.random.randint(part_keys[3], (TERMS,), 0, 3), jax.random.fold_in(part_keys[3], 1), 0, 2).astype(jnp.int32)
    sector_width = draw_sector_width(jax.random.fold_in(jax.random.fold_in(streams_of[5], part), 71), part)
    return {"wavefunction": wavefunction, "left_env": left_env, "right_env": right_env, "term_shift": term_shift, "sector_width": sector_width}


def by_term(environment):
    split_count = max(1, N_OP // TERMS)
    shaped = environment.reshape(split_count, TERMS, NSEC // split_count, B, B)
    return shaped.transpose(1, 2, 0, 3, 4).reshape(TERMS, NSEC, B, B)


def reference(wavefunction, left_env, right_env, term_shift, sector_width):
    zero_block = jnp.zeros((1,) + wavefunction.shape[1:], wavefunction.dtype)
    padded = jnp.concatenate([zero_block, wavefunction, zero_block], axis=0)
    sector_count = wavefunction.shape[0]
    left_terms = by_term(left_env)
    right_terms = by_term(right_env)

    def add_term(running, term_items):
        left_block, right_block, shift_value = term_items
        first_row = (2 - shift_value).astype(jnp.int32)
        source = lax.dynamic_slice_in_dim(padded, first_row, sector_count, 0)
        inner_block = jnp.einsum("qij,qvjk->qvik", left_block.astype(jnp.float32), source.astype(jnp.float32)).astype(jnp.bfloat16)
        return running + jnp.einsum("qvik,qlk->qvil", inner_block.astype(jnp.float32), right_block.astype(jnp.float32)), None

    start_total = jnp.zeros(wavefunction.shape, jnp.float32)
    summed, unused = lax.scan(add_term, start_total, (left_terms, right_terms, term_shift))
    line_index = jnp.arange(wavefunction.shape[2], dtype=jnp.int32)
    widths = sector_width[:, None, None]
    keep_mask = (line_index[None, :, None] < widths) & (line_index[None, None, :] < widths)
    return jnp.where(keep_mask[:, None], summed, jnp.float32(0.0))
```

```python
import functools

import jax
import jax.numpy as jnp
from jax import lax
from jax.experimental import pallas as pl
from jax.experimental.pallas import tpu as pltpu
from jax.sharding import PartitionSpec as P

TERMS = 32
MESH = pl.DeviceIdType.MESH


def kernel(
    n, slots, per,
    shift_ref, wave_ref, left_ref, right_ref,
    out_ref,
    lbuf, rbuf, xbuf, sbuf, gbuf,
    ag_send, ag_recv, rs_send, rs_recv, halo_send, halo_recv, env_local, env_send, env_recv, own_sem,
):
    half_ring = n // 2
    half = per // 2
    items = 2 * half_ring - 1
    group = lax.axis_index("groups")
    me = lax.axis_index("op")
    c = lax.rem(me, 2)
    chip = me // 2
    row = lax.rem(chip, 2)
    pos = (chip // 2) * (1 - row) + (n - 1 - chip // 2) * row

    def wrap(r):
        return lax.rem(r + 2 * n, n)

    def chip_at(r):
        side = r // half_ring
        return (r * (1 - side) + (n - 1 - r) * side) * 2 + side

    def ring_of(k):
        side = lax.rem(k, 2)
        return (k // 2) * (1 - side) + (n - 1 - k // 2) * side

    def dev(r):
        return (group, chip_at(r) * 2 + c)

    sibling = (group, chip * 2 + 1 - c)
    nexts = (dev(wrap(pos + 1)), dev(wrap(pos - 1)))
    signs = (1, -1)

    barrier = pltpu.get_barrier_semaphore()
    for target in (nexts[0], nexts[1], sibling):
        pl.semaphore_signal(barrier, inc=1, device_id=target, device_id_type=MESH)
    pl.semaphore_wait(barrier, 3)

    def half_of(d, k):
        parity = lax.rem(k, 2)
        return parity if d == 0 else 1 - parity

    def ag_copy(d, k, r, h, src=None):
        spot = xbuf.at[r, pl.ds(1 + h * half, half)]
        return pltpu.make_async_remote_copy(
            src_ref=spot if src is None else src, dst_ref=spot,
            send_sem=ag_send.at[d, k], recv_sem=ag_recv.at[d, k],
            device_id=nexts[d], device_id_type=MESH,
        )

    def halo_copy(r, h, src_row):
        goal = ring_of(wrap(chip_at(r) - (1 - c) * (1 - h) + c * h))
        return pltpu.make_async_remote_copy(
            src_ref=src_row, dst_ref=xbuf.at[goal, (per + 1) * (1 - h)],
            send_sem=halo_send.at[r, h], recv_sem=halo_recv.at[goal, h],
            device_id=sibling, device_id_type=MESH,
        )

    def halo_arrival(r, h):
        return pltpu.make_async_remote_copy(
            src_ref=xbuf.at[r, (per + 1) * (1 - h)], dst_ref=xbuf.at[r, (per + 1) * (1 - h)],
            send_sem=halo_send.at[r, h], recv_sem=halo_recv.at[r, h],
            device_id=sibling, device_id_type=MESH,
        )

    def env_copies():
        found = []
        for e, (src, dst) in enumerate(((left_ref, lbuf), (right_ref, rbuf))):
            mine = dst.at[pl.ds(c * slots, slots)]
            found.append((
                pltpu.make_async_copy(src.at[:, :, c], mine, env_local.at[e]),
                pltpu.make_async_remote_copy(
                    src_ref=src.at[:, :, 1 - c], dst_ref=mine,
                    send_sem=env_send.at[e], recv_sem=env_recv.at[e],
                    device_id=sibling, device_id_type=MESH,
                ),
                pltpu.make_async_remote_copy(
                    src_ref=src.at[:, :, 1 - c], dst_ref=dst.at[pl.ds((1 - c) * slots, slots)],
                    send_sem=env_send.at[e], recv_sem=env_recv.at[e],
                    device_id=sibling, device_id_type=MESH,
                ),
            ))
        return found

    for k in range(2):
        for d in range(2):
            h = k if d == 0 else 1 - k
            ag_copy(d, k, pos, h, wave_ref.at[pl.ds(h * half, half)]).start()
    own = pltpu.make_async_copy(wave_ref, xbuf.at[pos, pl.ds(1, per)], own_sem.at[0])
    own.start()
    for h in range(2):
        halo_copy(pos, h, wave_ref.at[h * (per - 1)]).start()
    for local, remote, _ in env_copies():
        local.start()
        remote.start()

    def gather_step(k, forward):
        for d in range(2):
            r = wrap(pos - signs[d] * (1 + k // 2))
            h = half_of(d, k)
            ag_copy(d, k, r, h).wait_recv()
            if forward:
                ag_copy(d, k + 2, r, h).start()
            halo_copy(r, h, xbuf.at[r, 1 + h * (per - 1)]).start()

    @pl.loop(0, items - 2)
    def _(k):
        gather_step(k, True)

    @pl.loop(items - 2, items)
    def _(k):
        gather_step(k, False)

    own.wait()
    for local, remote, arrival in env_copies():
        local.wait()
        arrival.wait_recv()

    @pl.loop(0, n)
    def _(r):
        for h in range(2):
            halo_arrival(r, h).wait_recv()

    xbuf[ring_of((n - 1) * c), (per + 1) * c] = jnp.zeros(xbuf.shape[2:], xbuf.dtype)

    vectors = wave_ref.shape[1]
    width = wave_ref.shape[2]

    def product(r, sector):
        k = chip_at(r)
        lines = [[] for _ in range(vectors)]
        rights = []
        for t in range(2 * slots):
            source = xbuf[r, sector + 2 - shift_ref[chip * 2 * slots + t]]
            side = jnp.concatenate([source[v] for v in range(vectors)], axis=1)
            inner = jnp.dot(lbuf[t, k, sector], side, preferred_element_type=jnp.float32)
            inner = inner.astype(jnp.bfloat16)
            for v in range(vectors):
                lines[v].append(inner[:, v * width:(v + 1) * width])
            rights.append(rbuf[t, k, sector])
        inner = jnp.concatenate([jnp.concatenate(line, axis=1) for line in lines], axis=0)
        total = lax.dot_general(
            inner, jnp.concatenate(rights, axis=1), (((1,), (1,)), ((), ())),
            preferred_element_type=jnp.float32,
        )
        return total.reshape((vectors, width, width))

    def rs_copy(d, k):
        return pltpu.make_async_remote_copy(
            src_ref=sbuf.at[d, k], dst_ref=gbuf.at[d, k],
            send_sem=rs_send.at[d, k], recv_sem=rs_recv.at[d, k],
            device_id=nexts[d], device_id_type=MESH,
        )

    def scatter_step(k, add):
        for d in range(2):
            r = wrap(pos + signs[d] * (half_ring - (k + 1) // 2))
            h = half_of(d, k)
            if add:
                rs_copy(d, k - 2).wait_recv()

            @pl.loop(0, half)
            def _(i):
                total = product(r, h * half + i)
                if add:
                    total = total + gbuf[d, k - 2, i].astype(jnp.float32)
                sbuf[d, k, i] = total.astype(jnp.bfloat16)

            rs_copy(d, k).start()

    @pl.loop(0, 2)
    def _(k):
        scatter_step(k, False)

    @pl.loop(2, items)
    def _(k):
        scatter_step(k, True)

    @pl.loop(0, per)
    def _(i):
        out_ref[i] = product(pos, i)

    for k in range(items - 2, items):
        for d in range(2):
            h = k % 2 if d == 0 else 1 - k % 2
            rs_copy(d, k).wait_recv()

            @pl.loop(0, half)
            def _(i):
                out_ref[h * half + i] = out_ref[h * half + i] + gbuf[d, k, i].astype(jnp.float32)

    @pl.loop(0, items)
    def _(k):
        for d in range(2):
            ag_copy(d, k, wrap(pos - signs[d] * (k // 2)), half_of(d, k)).wait_send()
            rs_copy(d, k).wait_send()

    @pl.loop(0, n)
    def _(r):
        for h in range(2):
            halo_copy(r, h, xbuf.at[r, 1 + h * (per - 1)]).wait_send()

    for _, remote, _ in env_copies():
        remote.wait_send()


def ring_sum(wavefunction, left_env, right_env, term_shift):
    n = lax.axis_size("op") // 2
    slots = left_env.shape[0]
    per, vectors, width, _ = wavefunction.shape
    items = 2 * (n // 2) - 1
    shaped = (slots, n, 2, per, width, width)
    env = (2 * slots, n, per, width, width)
    dma = pltpu.SemaphoreType.DMA
    work = 2 * slots * n * per * vectors * width ** 3 * 4
    return pl.pallas_call(
        functools.partial(kernel, n, slots, per),
        out_shape=jax.ShapeDtypeStruct(wavefunction.shape, jnp.float32),
        in_specs=[
            pl.BlockSpec(memory_space=pltpu.SMEM),
            pl.BlockSpec(memory_space=pl.ANY),
            pl.BlockSpec(memory_space=pl.ANY),
            pl.BlockSpec(memory_space=pl.ANY),
        ],
        out_specs=pl.BlockSpec(memory_space=pltpu.VMEM),
        scratch_shapes=[
            pltpu.VMEM(env, jnp.bfloat16),
            pltpu.VMEM(env, jnp.bfloat16),
            pltpu.VMEM((n, per + 2, vectors, width, width), jnp.bfloat16),
            pltpu.VMEM((2, items, per // 2, vectors, width, width), jnp.bfloat16),
            pltpu.VMEM((2, items, per // 2, vectors, width, width), jnp.bfloat16),
            dma((2, items)), dma((2, items)), dma((2, items)), dma((2, items)),
            dma((n, 2)), dma((n, 2)), dma((2,)), dma((2,)), dma((2,)), dma((1,)),
        ],
        compiler_params=pltpu.CompilerParams(
            collective_id=0, has_side_effects=True, vmem_limit_bytes=50 * 2 ** 20
        ),
        cost_estimate=pl.CostEstimate(flops=work, bytes_accessed=2 * left_env.size * 2, transcendentals=0),
    )(term_shift, wavefunction, left_env.reshape(shaped), right_env.reshape(shaped))


def gathered_sum(wavefunction, left_env, right_env, term_shift):
    devices = lax.axis_size("op")
    split_count = max(1, devices // TERMS)
    slot_dev = left_env.shape[0]
    half_sec = left_env.shape[1]
    block_tail = wavefunction.shape[1:]
    gathered = lax.all_gather(wavefunction, "op", axis=0, tiled=True)
    zero_block = jnp.zeros((1,) + block_tail, gathered.dtype)
    padded = jnp.concatenate([zero_block, gathered, zero_block], axis=0)
    my_index = lax.axis_index("op")
    places = jnp.arange(half_sec, dtype=jnp.int32)
    partial_value = jnp.zeros((half_sec,) + block_tail, jnp.float32)
    for slot_index in range(slot_dev):
        slot_rank = my_index * slot_dev + slot_index
        half_index = slot_rank // TERMS
        term_index = slot_rank % TERMS
        shift_value = term_shift[term_index] - 1
        row_index = places * split_count + half_index - shift_value + 1
        source = jnp.take(padded, row_index, axis=0)
        inner_block = jnp.einsum(
            "qij,qvjk->qvik", left_env[slot_index], source, preferred_element_type=jnp.float32
        ).astype(jnp.bfloat16)
        partial_value = partial_value + jnp.einsum(
            "qvik,qlk->qvil", inner_block, right_env[slot_index], preferred_element_type=jnp.float32
        )
    arrived = lax.all_to_all(partial_value, "op", split_axis=0, concat_axis=0, tiled=True)
    per_peer = half_sec // devices
    grouped = arrived.reshape((split_count, devices // split_count, per_peer) + block_tail)
    summed = jnp.sum(grouped, axis=1)
    return jnp.swapaxes(summed, 0, 1).reshape(wavefunction.shape)


def per_device(wavefunction, left_env, right_env, term_shift, sector_width):
    devices = lax.axis_size("op")
    fits = devices <= TERMS and devices % 4 == 0 and devices >= 8 and wavefunction.shape[0] % 2 == 0
    combine = ring_sum if fits else gathered_sum
    summed = combine(wavefunction, left_env, right_env, term_shift)
    line_index = jnp.arange(wavefunction.shape[2], dtype=jnp.int32)
    widths = sector_width[:, None, None]
    keep_mask = (line_index[None, :, None] < widths) & (line_index[None, None, :] < widths)
    return jnp.where(keep_mask[:, None], summed, jnp.float32(0.0))


def solution(mesh):
    return jax.shard_map(
        per_device,
        mesh=mesh,
        in_specs=(
            P(("groups", "op"), None, None, None),
            P(("groups", "op"), None, None, None),
            P(("groups", "op"), None, None, None),
            P("groups"),
            P(("groups", "op")),
        ),
        out_specs=P(("groups", "op"), None, None, None),
        check_vma=False,
    )
```

```python
import functools

import jax
import jax.numpy as jnp
from jax import lax
from jax.experimental import pallas as pl
from jax.experimental.pallas import tpu as pltpu
from jax.sharding import PartitionSpec as P

TERMS = 32
MESH = pl.DeviceIdType.MESH


def kernel(
    n, slots, per,
    shift_ref, live_ref, wave_ref, left_ref, right_ref,
    out_ref,
    lbuf, rbuf, xbuf, sbuf, gbuf,
    ag_send, ag_recv, rs_send, rs_recv, halo_send, halo_recv, env_local, env_send, env_recv, own_sem,
    head_send, head_recv,
):
    half_ring = n // 2
    half = per // 2
    items = 2 * half_ring - 1
    group = lax.axis_index("groups")
    me = lax.axis_index("op")
    c = lax.rem(me, 2)
    chip = me // 2
    row = lax.rem(chip, 2)
    pos = (chip // 2) * (1 - row) + (n - 1 - chip // 2) * row

    def wrap(r):
        return lax.rem(r + 2 * n, n)

    def chip_at(r):
        side = r // half_ring
        return (r * (1 - side) + (n - 1 - r) * side) * 2 + side

    def ring_of(k):
        side = lax.rem(k, 2)
        return (k // 2) * (1 - side) + (n - 1 - k // 2) * side

    def dev(r):
        return (group, chip_at(r) * 2 + c)

    sibling = (group, chip * 2 + 1 - c)
    nexts = (dev(wrap(pos + 1)), dev(wrap(pos - 1)))
    signs = (1, -1)

    barrier = pltpu.get_barrier_semaphore()
    for target in (nexts[0], nexts[1], sibling):
        pl.semaphore_signal(barrier, inc=1, device_id=target, device_id_type=MESH)
    pl.semaphore_wait(barrier, 3)

    def half_of(d, k):
        parity = k % 2 if isinstance(k, int) else lax.rem(k, 2)
        return parity if d == 0 else 1 - parity

    def ag_copy(d, k, r, h, src=None):
        spot = xbuf.at[r, pl.ds(1 + h * half, half)]
        return pltpu.make_async_remote_copy(
            src_ref=spot if src is None else src, dst_ref=spot,
            send_sem=ag_send.at[d, k], recv_sem=ag_recv.at[d, k],
            device_id=nexts[d], device_id_type=MESH,
        )

    def halo_copy(r, h, src_row):
        goal = ring_of(wrap(chip_at(r) - (1 - c) * (1 - h) + c * h))
        return pltpu.make_async_remote_copy(
            src_ref=src_row, dst_ref=xbuf.at[goal, (per + 1) * (1 - h)],
            send_sem=halo_send.at[r, h], recv_sem=halo_recv.at[goal, h],
            device_id=sibling, device_id_type=MESH,
        )

    def halo_arrival(r, h):
        return pltpu.make_async_remote_copy(
            src_ref=xbuf.at[r, (per + 1) * (1 - h)], dst_ref=xbuf.at[r, (per + 1) * (1 - h)],
            send_sem=halo_send.at[r, h], recv_sem=halo_recv.at[r, h],
            device_id=sibling, device_id_type=MESH,
        )

    def env_copies():
        found = []
        for e, (src, dst) in enumerate(((left_ref, lbuf), (right_ref, rbuf))):
            mine = dst.at[pl.ds(c * slots, slots)]
            found.append((
                pltpu.make_async_copy(src.at[:, :, c], mine, env_local.at[e]),
                pltpu.make_async_remote_copy(
                    src_ref=src.at[:, :, 1 - c], dst_ref=mine,
                    send_sem=env_send.at[e], recv_sem=env_recv.at[e],
                    device_id=sibling, device_id_type=MESH,
                ),
                pltpu.make_async_remote_copy(
                    src_ref=src.at[:, :, 1 - c], dst_ref=dst.at[pl.ds((1 - c) * slots, slots)],
                    send_sem=env_send.at[e], recv_sem=env_recv.at[e],
                    device_id=sibling, device_id_type=MESH,
                ),
            ))
        return found

    for k in range(2):
        for d in range(2):
            h = k if d == 0 else 1 - k
            ag_copy(d, k, pos, h, wave_ref.at[pl.ds(h * half, half)]).start()
    own = pltpu.make_async_copy(wave_ref, xbuf.at[pos, pl.ds(1, per)], own_sem.at[0])
    own.start()
    for h in range(2):
        halo_copy(pos, h, wave_ref.at[h * (per - 1)]).start()
    for local, remote, _ in env_copies():
        local.start()
        remote.start()

    def gather_step(k, forward):
        for d in range(2):
            r = wrap(pos - signs[d] * (1 + k // 2))
            h = half_of(d, k)
            ag_copy(d, k, r, h).wait_recv()
            if forward:
                ag_copy(d, k + 2, r, h).start()
            halo_copy(r, h, xbuf.at[r, 1 + h * (per - 1)]).start()

    @pl.loop(0, items - 2)
    def _(k):
        gather_step(k, True)

    @pl.loop(items - 2, items)
    def _(k):
        gather_step(k, False)

    own.wait()
    for local, remote, arrival in env_copies():
        local.wait()
        arrival.wait_recv()

    @pl.loop(0, n)
    def _(r):
        for h in range(2):
            halo_arrival(r, h).wait_recv()

    xbuf[ring_of((n - 1) * c), (per + 1) * c] = jnp.zeros(xbuf.shape[2:], xbuf.dtype)

    vectors = wave_ref.shape[1]
    width = wave_ref.shape[2]

    def product(r, sector):
        k = chip_at(r)
        lines = [[] for _ in range(vectors)]
        rights = []
        for t in range(2 * slots):
            source = xbuf[r, sector + 2 - shift_ref[chip * 2 * slots + t]]
            side = jnp.concatenate([source[v] for v in range(vectors)], axis=1)
            inner = jnp.dot(lbuf[t, k, sector], side, preferred_element_type=jnp.float32)
            inner = inner.astype(jnp.bfloat16)
            for v in range(vectors):
                lines[v].append(inner[:, v * width:(v + 1) * width])
            rights.append(rbuf[t, k, sector])
        inner = jnp.concatenate([jnp.concatenate(line, axis=1) for line in lines], axis=0)
        total = lax.dot_general(
            inner, jnp.concatenate(rights, axis=1), (((1,), (1,)), ((), ())),
            preferred_element_type=jnp.float32,
        )
        return total.reshape((vectors, width, width))

    def rs_copy(d, k):
        return pltpu.make_async_remote_copy(
            src_ref=sbuf.at[d, k], dst_ref=gbuf.at[d, k],
            send_sem=rs_send.at[d, k], recv_sem=rs_recv.at[d, k],
            device_id=nexts[d], device_id_type=MESH,
        )

    def scatter_step(k, add):
        for d in range(2):
            r = wrap(pos + signs[d] * (half_ring - (k + 1) // 2))
            h = half_of(d, k)
            if isinstance(k, int) and k == 2:
                @pl.loop(0, half)
                def _(i):
                    head_copy(d, i).wait_recv()
            elif add:
                rs_copy(d, k - 2).wait_recv()

            @pl.loop(0, half)
            def _(i):
                total = product(r, h * half + i)
                if add:
                    total = total + gbuf[d, k - 2, i].astype(jnp.float32)
                sbuf[d, k, i] = total.astype(jnp.bfloat16)

            rs_copy(d, k).start()

    def head_copy(d, i):
        return pltpu.make_async_remote_copy(
            src_ref=sbuf.at[d, 0, i], dst_ref=gbuf.at[d, 0, i],
            send_sem=head_send.at[d, i], recv_sem=head_recv.at[d, i],
            device_id=nexts[d], device_id_type=MESH,
        )

    @pl.loop(0, half)
    def _(i):
        for d in range(2):
            r = wrap(pos + signs[d] * half_ring)
            sbuf[d, 0, i] = product(r, d * half + i).astype(jnp.bfloat16)
            head_copy(d, i).start()

    scatter_step(1, False)
    scatter_step(2, True)

    @pl.loop(3, items)
    def _(k):
        scatter_step(k, True)

    @pl.loop(0, per)
    def _(i):
        out_ref[i] = product(pos, i)

    for k in range(items - 2, items):
        for d in range(2):
            h = k % 2 if d == 0 else 1 - k % 2
            rs_copy(d, k).wait_recv()

            @pl.loop(0, half)
            def _(i):
                value = out_ref[h * half + i] + gbuf[d, k, i].astype(jnp.float32)
                if k == items - 1:
                    live = live_ref[h * half + i]
                    down = lax.broadcasted_iota(jnp.int32, (width, width), 0)
                    along = lax.broadcasted_iota(jnp.int32, (width, width), 1)
                    keep = ((down < live) & (along < live))[None]
                    value = jnp.where(keep, value, jnp.float32(0.0))
                out_ref[h * half + i] = value

    @pl.loop(0, items)
    def _(k):
        for d in range(2):
            ag_copy(d, k, wrap(pos - signs[d] * (k // 2)), half_of(d, k)).wait_send()

    @pl.loop(1, items)
    def _(k):
        for d in range(2):
            rs_copy(d, k).wait_send()

    @pl.loop(0, half)
    def _(i):
        for d in range(2):
            head_copy(d, i).wait_send()

    @pl.loop(0, n)
    def _(r):
        for h in range(2):
            halo_copy(r, h, xbuf.at[r, 1 + h * (per - 1)]).wait_send()

    for _, remote, _ in env_copies():
        remote.wait_send()


def ring_sum(wavefunction, left_env, right_env, term_shift, sector_width):
    n = lax.axis_size("op") // 2
    slots = left_env.shape[0]
    per, vectors, width, _ = wavefunction.shape
    items = 2 * (n // 2) - 1
    shaped = (slots, n, 2, per, width, width)
    env = (2 * slots, n, per, width, width)
    dma = pltpu.SemaphoreType.DMA
    work = 2 * slots * n * per * vectors * width ** 3 * 4
    return pl.pallas_call(
        functools.partial(kernel, n, slots, per),
        out_shape=jax.ShapeDtypeStruct(wavefunction.shape, jnp.float32),
        in_specs=[
            pl.BlockSpec(memory_space=pltpu.SMEM),
            pl.BlockSpec(memory_space=pltpu.SMEM),
            pl.BlockSpec(memory_space=pl.ANY),
            pl.BlockSpec(memory_space=pl.ANY),
            pl.BlockSpec(memory_space=pl.ANY),
        ],
        out_specs=pl.BlockSpec(memory_space=pltpu.VMEM),
        scratch_shapes=[
            pltpu.VMEM(env, jnp.bfloat16),
            pltpu.VMEM(env, jnp.bfloat16),
            pltpu.VMEM((n, per + 2, vectors, width, width), jnp.bfloat16),
            pltpu.VMEM((2, items, per // 2, vectors, width, width), jnp.bfloat16),
            pltpu.VMEM((2, items, per // 2, vectors, width, width), jnp.bfloat16),
            dma((2, items)), dma((2, items)), dma((2, items)), dma((2, items)),
            dma((n, 2)), dma((n, 2)), dma((2,)), dma((2,)), dma((2,)), dma((1,)),
            dma((2, per // 2)), dma((2, per // 2)),
        ],
        compiler_params=pltpu.CompilerParams(
            collective_id=0, has_side_effects=True, vmem_limit_bytes=60 * 2 ** 20
        ),
        cost_estimate=pl.CostEstimate(flops=work, bytes_accessed=2 * left_env.size * 2, transcendentals=0),
    )(term_shift, sector_width, wavefunction, left_env.reshape(shaped), right_env.reshape(shaped))


def gathered_sum(wavefunction, left_env, right_env, term_shift):
    devices = lax.axis_size("op")
    split_count = max(1, devices // TERMS)
    slot_dev = left_env.shape[0]
    half_sec = left_env.shape[1]
    block_tail = wavefunction.shape[1:]
    gathered = lax.all_gather(wavefunction, "op", axis=0, tiled=True)
    zero_block = jnp.zeros((1,) + block_tail, gathered.dtype)
    padded = jnp.concatenate([zero_block, gathered, zero_block], axis=0)
    my_index = lax.axis_index("op")
    places = jnp.arange(half_sec, dtype=jnp.int32)
    partial_value = jnp.zeros((half_sec,) + block_tail, jnp.float32)
    for slot_index in range(slot_dev):
        slot_rank = my_index * slot_dev + slot_index
        half_index = slot_rank // TERMS
        term_index = slot_rank % TERMS
        shift_value = term_shift[term_index] - 1
        row_index = places * split_count + half_index - shift_value + 1
        source = jnp.take(padded, row_index, axis=0)
        inner_block = jnp.einsum(
            "qij,qvjk->qvik", left_env[slot_index], source, preferred_element_type=jnp.float32
        ).astype(jnp.bfloat16)
        partial_value = partial_value + jnp.einsum(
            "qvik,qlk->qvil", inner_block, right_env[slot_index], preferred_element_type=jnp.float32
        )
    arrived = lax.all_to_all(partial_value, "op", split_axis=0, concat_axis=0, tiled=True)
    per_peer = half_sec // devices
    grouped = arrived.reshape((split_count, devices // split_count, per_peer) + block_tail)
    summed = jnp.sum(grouped, axis=1)
    return jnp.swapaxes(summed, 0, 1).reshape(wavefunction.shape)


def per_device(wavefunction, left_env, right_env, term_shift, sector_width):
    devices = lax.axis_size("op")
    fits = devices <= TERMS and devices % 4 == 0 and devices >= 8 and wavefunction.shape[0] % 2 == 0
    if fits:
        return ring_sum(wavefunction, left_env, right_env, term_shift, sector_width)
    summed = gathered_sum(wavefunction, left_env, right_env, term_shift)
    line_index = jnp.arange(wavefunction.shape[2], dtype=jnp.int32)
    widths = sector_width[:, None, None]
    keep_mask = (line_index[None, :, None] < widths) & (line_index[None, None, :] < widths)
    return jnp.where(keep_mask[:, None], summed, jnp.float32(0.0))


def solution(mesh):
    return jax.shard_map(
        per_device,
        mesh=mesh,
        in_specs=(
            P(("groups", "op"), None, None, None),
            P(("groups", "op"), None, None, None),
            P(("groups", "op"), None, None, None),
            P("groups"),
            P(("groups", "op")),
        ),
        out_specs=P(("groups", "op"), None, None, None),
        check_vma=False,
    )
```

```python
import functools

import jax
import jax.numpy as jnp
from jax import lax
from jax.experimental import pallas as pl
from jax.experimental.pallas import tpu as pltpu
from jax.sharding import PartitionSpec as P

TERMS = 32
MESH = pl.DeviceIdType.MESH


def kernel(
    n, slots, per,
    shift_ref, live_ref, wave_ref, left_ref, right_ref,
    out_ref,
    lbuf, rbuf, xbuf, sbuf, gbuf,
    ag_send, ag_recv, rs_send, rs_recv, halo_send, halo_recv, env_local, env_send, env_recv, own_sem,
    head_send, head_recv,
):
    half_ring = n // 2
    half = per // 2
    items = 2 * half_ring - 1
    group = lax.axis_index("groups")
    me = lax.axis_index("op")
    c = lax.rem(me, 2)
    chip = me // 2
    row = lax.rem(chip, 2)
    pos = (chip // 2) * (1 - row) + (n - 1 - chip // 2) * row

    def wrap(r):
        return lax.rem(r + 2 * n, n)

    def chip_at(r):
        side = r // half_ring
        return (r * (1 - side) + (n - 1 - r) * side) * 2 + side

    def ring_of(k):
        side = lax.rem(k, 2)
        return (k // 2) * (1 - side) + (n - 1 - k // 2) * side

    def dev(r):
        return (group, chip_at(r) * 2 + c)

    sibling = (group, chip * 2 + 1 - c)
    nexts = (dev(wrap(pos + 1)), dev(wrap(pos - 1)))
    signs = (1, -1)

    barrier = pltpu.get_barrier_semaphore()
    for target in (nexts[0], nexts[1], sibling):
        pl.semaphore_signal(barrier, inc=1, device_id=target, device_id_type=MESH)
    pl.semaphore_wait(barrier, 3)

    def half_of(d, k):
        parity = k % 2 if isinstance(k, int) else lax.rem(k, 2)
        return parity if d == 0 else 1 - parity

    def ag_copy(d, k, r, h, src=None):
        spot = xbuf.at[r, pl.ds(1 + h * half, half)]
        return pltpu.make_async_remote_copy(
            src_ref=spot if src is None else src, dst_ref=spot,
            send_sem=ag_send.at[d, k], recv_sem=ag_recv.at[d, k],
            device_id=nexts[d], device_id_type=MESH,
        )

    def halo_copy(r, h, src_row):
        goal = ring_of(wrap(chip_at(r) - (1 - c) * (1 - h) + c * h))
        return pltpu.make_async_remote_copy(
            src_ref=src_row, dst_ref=xbuf.at[goal, (per + 1) * (1 - h)],
            send_sem=halo_send.at[r, h], recv_sem=halo_recv.at[goal, h],
            device_id=sibling, device_id_type=MESH,
        )

    def halo_arrival(r, h):
        return pltpu.make_async_remote_copy(
            src_ref=xbuf.at[r, (per + 1) * (1 - h)], dst_ref=xbuf.at[r, (per + 1) * (1 - h)],
            send_sem=halo_send.at[r, h], recv_sem=halo_recv.at[r, h],
            device_id=sibling, device_id_type=MESH,
        )

    def env_copies():
        found = []
        for e, (src, dst) in enumerate(((left_ref, lbuf), (right_ref, rbuf))):
            mine = dst.at[pl.ds(c * slots, slots)]
            found.append((
                pltpu.make_async_copy(src.at[:, :, c], mine, env_local.at[e]),
                pltpu.make_async_remote_copy(
                    src_ref=src.at[:, :, 1 - c], dst_ref=mine,
                    send_sem=env_send.at[e], recv_sem=env_recv.at[e],
                    device_id=sibling, device_id_type=MESH,
                ),
                pltpu.make_async_remote_copy(
                    src_ref=src.at[:, :, 1 - c], dst_ref=dst.at[pl.ds((1 - c) * slots, slots)],
                    send_sem=env_send.at[e], recv_sem=env_recv.at[e],
                    device_id=sibling, device_id_type=MESH,
                ),
            ))
        return found

    for k in range(2):
        for d in range(2):
            h = k if d == 0 else 1 - k
            ag_copy(d, k, pos, h, wave_ref.at[pl.ds(h * half, half)]).start()
    own = pltpu.make_async_copy(wave_ref, xbuf.at[pos, pl.ds(1, per)], own_sem.at[0])
    own.start()
    for h in range(2):
        halo_copy(pos, h, wave_ref.at[h * (per - 1)]).start()
    for local, remote, _ in env_copies():
        local.start()
        remote.start()

    def gather_step(k, forward):
        for d in range(2):
            r = wrap(pos - signs[d] * (1 + k // 2))
            h = half_of(d, k)
            ag_copy(d, k, r, h).wait_recv()
            if forward:
                ag_copy(d, k + 2, r, h).start()
            halo_copy(r, h, xbuf.at[r, 1 + h * (per - 1)]).start()

    @pl.loop(0, items - 2)
    def _(k):
        gather_step(k, True)

    @pl.loop(items - 2, items)
    def _(k):
        gather_step(k, False)

    own.wait()
    for local, remote, arrival in env_copies():
        local.wait()
        arrival.wait_recv()

    @pl.loop(0, n)
    def _(r):
        for h in range(2):
            halo_arrival(r, h).wait_recv()

    xbuf[ring_of((n - 1) * c), (per + 1) * c] = jnp.zeros(xbuf.shape[2:], xbuf.dtype)

    vectors = wave_ref.shape[1]
    width = wave_ref.shape[2]

    def product(r, sector):
        k = chip_at(r)
        lines = [[] for _ in range(vectors)]
        rights = []
        for t in range(2 * slots):
            source = xbuf[r, sector + 2 - shift_ref[chip * 2 * slots + t]]
            side = jnp.concatenate([source[v] for v in range(vectors)], axis=1)
            inner = jnp.dot(lbuf[t, k, sector], side, preferred_element_type=jnp.float32)
            inner = inner.astype(jnp.bfloat16)
            for v in range(vectors):
                lines[v].append(inner[:, v * width:(v + 1) * width])
            rights.append(rbuf[t, k, sector])
        inner = jnp.concatenate([jnp.concatenate(line, axis=1) for line in lines], axis=0)
        total = lax.dot_general(
            inner, jnp.concatenate(rights, axis=1), (((1,), (1,)), ((), ())),
            preferred_element_type=jnp.float32,
        )
        return total.reshape((vectors, width, width))

    def rs_copy(d, k):
        return pltpu.make_async_remote_copy(
            src_ref=sbuf.at[d, k], dst_ref=gbuf.at[d, k],
            send_sem=rs_send.at[d, k], recv_sem=rs_recv.at[d, k],
            device_id=nexts[d], device_id_type=MESH,
        )

    def scatter_step(k, add):
        for d in range(2):
            r = wrap(pos + signs[d] * (half_ring - (k + 1) // 2))
            h = half_of(d, k)
            if isinstance(k, int) and k == 2:
                @pl.loop(0, half)
                def _(i):
                    head_copy(d, i).wait_recv()
            elif add:
                rs_copy(d, k - 2).wait_recv()

            @pl.loop(0, half)
            def _(i):
                total = product(r, h * half + i)
                if add:
                    total = total + gbuf[d, k - 2, i].astype(jnp.float32)
                sbuf[d, k, i] = total.astype(jnp.bfloat16)

            rs_copy(d, k).start()

    def head_copy(d, i):
        return pltpu.make_async_remote_copy(
            src_ref=sbuf.at[d, 0, i], dst_ref=gbuf.at[d, 0, i],
            send_sem=head_send.at[d, i], recv_sem=head_recv.at[d, i],
            device_id=nexts[d], device_id_type=MESH,
        )

    @pl.loop(0, half)
    def _(i):
        for d in range(2):
            r = wrap(pos + signs[d] * half_ring)
            sbuf[d, 0, i] = product(r, d * half + i).astype(jnp.bfloat16)
            head_copy(d, i).start()

    scatter_step(1, False)
    scatter_step(2, True)

    @pl.loop(3, items)
    def _(k):
        scatter_step(k, True)

    @pl.loop(0, per)
    def _(i):
        out_ref[i] = product(pos, i)

    for k in range(items - 2, items):
        for d in range(2):
            h = k % 2 if d == 0 else 1 - k % 2
            rs_copy(d, k).wait_recv()

            @pl.loop(0, half)
            def _(i):
                value = out_ref[h * half + i] + gbuf[d, k, i].astype(jnp.float32)
                if k == items - 1:
                    live = live_ref[h * half + i]
                    down = lax.broadcasted_iota(jnp.int32, (width, width), 0)
                    along = lax.broadcasted_iota(jnp.int32, (width, width), 1)
                    keep = ((down < live) & (along < live))[None]
                    value = jnp.where(keep, value, jnp.float32(0.0))
                out_ref[h * half + i] = value

    @pl.loop(0, items)
    def _(k):
        for d in range(2):
            ag_copy(d, k, wrap(pos - signs[d] * (k // 2)), half_of(d, k)).wait_send()

    @pl.loop(1, items)
    def _(k):
        for d in range(2):
            rs_copy(d, k).wait_send()

    @pl.loop(0, half)
    def _(i):
        for d in range(2):
            head_copy(d, i).wait_send()

    @pl.loop(0, n)
    def _(r):
        for h in range(2):
            halo_copy(r, h, xbuf.at[r, 1 + h * (per - 1)]).wait_send()

    for _, remote, _ in env_copies():
        remote.wait_send()


def ring_sum(wavefunction, left_env, right_env, term_shift, sector_width):
    n = lax.axis_size("op") // 2
    slots = left_env.shape[0]
    per, vectors, width, _ = wavefunction.shape
    items = 2 * (n // 2) - 1
    shaped = (slots, n, 2, per, width, width)
    env = (2 * slots, n, per, width, width)
    dma = pltpu.SemaphoreType.DMA
    work = 2 * slots * n * per * vectors * width ** 3 * 4
    return pl.pallas_call(
        functools.partial(kernel, n, slots, per),
        out_shape=jax.ShapeDtypeStruct(wavefunction.shape, jnp.float32),
        in_specs=[
            pl.BlockSpec(memory_space=pltpu.SMEM),
            pl.BlockSpec(memory_space=pltpu.SMEM),
            pl.BlockSpec(memory_space=pltpu.HBM),
            pl.BlockSpec(memory_space=pltpu.HBM),
            pl.BlockSpec(memory_space=pltpu.HBM),
        ],
        out_specs=pl.BlockSpec(memory_space=pltpu.VMEM),
        scratch_shapes=[
            pltpu.VMEM(env, jnp.bfloat16),
            pltpu.VMEM(env, jnp.bfloat16),
            pltpu.VMEM((n, per + 2, vectors, width, width), jnp.bfloat16),
            pltpu.VMEM((2, items, per // 2, vectors, width, width), jnp.bfloat16),
            pltpu.VMEM((2, items, per // 2, vectors, width, width), jnp.bfloat16),
            dma((2, items)), dma((2, items)), dma((2, items)), dma((2, items)),
            dma((n, 2)), dma((n, 2)), dma((2,)), dma((2,)), dma((2,)), dma((1,)),
            dma((2, per // 2)), dma((2, per // 2)),
        ],
        compiler_params=pltpu.CompilerParams(
            collective_id=0, has_side_effects=True, vmem_limit_bytes=48 * 2 ** 20
        ),
        cost_estimate=pl.CostEstimate(flops=work, bytes_accessed=2 * left_env.size * 2, transcendentals=0),
    )(term_shift, sector_width, wavefunction, left_env.reshape(shaped), right_env.reshape(shaped))


def gathered_sum(wavefunction, left_env, right_env, term_shift):
    devices = lax.axis_size("op")
    split_count = max(1, devices // TERMS)
    slot_dev = left_env.shape[0]
    half_sec = left_env.shape[1]
    block_tail = wavefunction.shape[1:]
    gathered = lax.all_gather(wavefunction, "op", axis=0, tiled=True)
    zero_block = jnp.zeros((1,) + block_tail, gathered.dtype)
    padded = jnp.concatenate([zero_block, gathered, zero_block], axis=0)
    my_index = lax.axis_index("op")
    places = jnp.arange(half_sec, dtype=jnp.int32)
    partial_value = jnp.zeros((half_sec,) + block_tail, jnp.float32)
    for slot_index in range(slot_dev):
        slot_rank = my_index * slot_dev + slot_index
        half_index = slot_rank // TERMS
        term_index = slot_rank % TERMS
        shift_value = term_shift[term_index] - 1
        row_index = places * split_count + half_index - shift_value + 1
        source = jnp.take(padded, row_index, axis=0)
        inner_block = jnp.einsum(
            "qij,qvjk->qvik", left_env[slot_index], source, preferred_element_type=jnp.float32
        ).astype(jnp.bfloat16)
        partial_value = partial_value + jnp.einsum(
            "qvik,qlk->qvil", inner_block, right_env[slot_index], preferred_element_type=jnp.float32
        )
    arrived = lax.all_to_all(partial_value, "op", split_axis=0, concat_axis=0, tiled=True)
    per_peer = half_sec // devices
    grouped = arrived.reshape((split_count, devices // split_count, per_peer) + block_tail)
    summed = jnp.sum(grouped, axis=1)
    return jnp.swapaxes(summed, 0, 1).reshape(wavefunction.shape)


def per_device(wavefunction, left_env, right_env, term_shift, sector_width):
    devices = lax.axis_size("op")
    fits = devices <= TERMS and devices % 4 == 0 and devices >= 8 and wavefunction.shape[0] % 2 == 0
    if fits:
        return ring_sum(wavefunction, left_env, right_env, term_shift, sector_width)
    summed = gathered_sum(wavefunction, left_env, right_env, term_shift)
    line_index = jnp.arange(wavefunction.shape[2], dtype=jnp.int32)
    widths = sector_width[:, None, None]
    keep_mask = (line_index[None, :, None] < widths) & (line_index[None, None, :] < widths)
    return jnp.where(keep_mask[:, None], summed, jnp.float32(0.0))


def solution(mesh):
    return jax.shard_map(
        per_device,
        mesh=mesh,
        in_specs=(
            P(("groups", "op"), None, None, None),
            P(("groups", "op"), None, None, None),
            P(("groups", "op"), None, None, None),
            P("groups"),
            P(("groups", "op")),
        ),
        out_specs=P(("groups", "op"), None, None, None),
        check_vma=False,
    )
```

```python
import functools

import jax
import jax.numpy as jnp
from jax import lax
from jax.experimental import pallas as pl
from jax.experimental.pallas import tpu as pltpu
from jax.sharding import PartitionSpec as P

TERMS = 32
MESH = pl.DeviceIdType.MESH


def kernel(
    n, slots, per,
    shift_ref, live_ref, wave_ref, left_ref, right_ref,
    out_ref,
    lbuf, rbuf, xbuf, sbuf, gbuf,
    ag_send, ag_recv, rs_send, rs_recv, halo_send, halo_recv, env_local, env_send, env_recv, own_sem,
    head_send, head_recv,
):
    half_ring = n // 2
    half = per // 2
    items = 2 * half_ring - 1
    group = lax.axis_index("groups")
    me = lax.axis_index("op")
    c = lax.rem(me, 2)
    chip = me // 2
    row = lax.rem(chip, 2)
    pos = (chip // 2) * (1 - row) + (n - 1 - chip // 2) * row

    def wrap(r):
        return lax.rem(r + 2 * n, n)

    def chip_at(r):
        side = r // half_ring
        return (r * (1 - side) + (n - 1 - r) * side) * 2 + side

    def ring_of(k):
        side = lax.rem(k, 2)
        return (k // 2) * (1 - side) + (n - 1 - k // 2) * side

    def dev(r):
        return (group, chip_at(r) * 2 + c)

    sibling = (group, chip * 2 + 1 - c)
    nexts = (dev(wrap(pos + 1)), dev(wrap(pos - 1)))
    signs = (1, -1)

    barrier = pltpu.get_barrier_semaphore()
    for target in (nexts[0], nexts[1], sibling):
        pl.semaphore_signal(barrier, inc=1, device_id=target, device_id_type=MESH)
    pl.semaphore_wait(barrier, 3)

    def half_of(d, k):
        parity = k % 2 if isinstance(k, int) else lax.rem(k, 2)
        return parity if d == 0 else 1 - parity

    def ag_copy(d, k, r, h, src=None):
        spot = xbuf.at[r, pl.ds(1 + h * half, half)]
        return pltpu.make_async_remote_copy(
            src_ref=spot if src is None else src, dst_ref=spot,
            send_sem=ag_send.at[d, k], recv_sem=ag_recv.at[d, k],
            device_id=nexts[d], device_id_type=MESH,
        )

    def halo_copy(r, h, src_row):
        goal = ring_of(wrap(chip_at(r) - (1 - c) * (1 - h) + c * h))
        return pltpu.make_async_remote_copy(
            src_ref=src_row, dst_ref=xbuf.at[goal, (per + 1) * (1 - h)],
            send_sem=halo_send.at[r, h], recv_sem=halo_recv.at[goal, h],
            device_id=sibling, device_id_type=MESH,
        )

    def halo_arrival(r, h):
        return pltpu.make_async_remote_copy(
            src_ref=xbuf.at[r, (per + 1) * (1 - h)], dst_ref=xbuf.at[r, (per + 1) * (1 - h)],
            send_sem=halo_send.at[r, h], recv_sem=halo_recv.at[r, h],
            device_id=sibling, device_id_type=MESH,
        )

    def env_copies():
        found = []
        for e, (src, dst) in enumerate(((left_ref, lbuf), (right_ref, rbuf))):
            mine = dst.at[pl.ds(c * slots, slots)]
            found.append((
                pltpu.make_async_copy(src.at[:, :, c], mine, env_local.at[e]),
                pltpu.make_async_remote_copy(
                    src_ref=src.at[:, :, 1 - c], dst_ref=mine,
                    send_sem=env_send.at[e], recv_sem=env_recv.at[e],
                    device_id=sibling, device_id_type=MESH,
                ),
                pltpu.make_async_remote_copy(
                    src_ref=src.at[:, :, 1 - c], dst_ref=dst.at[pl.ds((1 - c) * slots, slots)],
                    send_sem=env_send.at[e], recv_sem=env_recv.at[e],
                    device_id=sibling, device_id_type=MESH,
                ),
            ))
        return found

    for k in range(2):
        for d in range(2):
            h = k if d == 0 else 1 - k
            ag_copy(d, k, pos, h, wave_ref.at[pl.ds(h * half, half)]).start()
    own = pltpu.make_async_copy(wave_ref, xbuf.at[pos, pl.ds(1, per)], own_sem.at[0])
    own.start()
    for h in range(2):
        halo_copy(pos, h, wave_ref.at[h * (per - 1)]).start()
    for local, remote, _ in env_copies():
        local.start()
        remote.start()

    def gather_step(k, forward):
        for d in range(2):
            r = wrap(pos - signs[d] * (1 + k // 2))
            h = half_of(d, k)
            ag_copy(d, k, r, h).wait_recv()
            if forward:
                ag_copy(d, k + 2, r, h).start()
            halo_copy(r, h, xbuf.at[r, 1 + h * (per - 1)]).start()

    @pl.loop(0, items - 2)
    def _(k):
        gather_step(k, True)

    @pl.loop(items - 2, items)
    def _(k):
        gather_step(k, False)

    own.wait()
    for local, remote, arrival in env_copies():
        local.wait()
        arrival.wait_recv()

    @pl.loop(0, n)
    def _(r):
        for h in range(2):
            halo_arrival(r, h).wait_recv()

    xbuf[ring_of((n - 1) * c), (per + 1) * c] = jnp.zeros(xbuf.shape[2:], xbuf.dtype)

    vectors = wave_ref.shape[1]
    width = wave_ref.shape[2]

    def product(r, sector):
        k = chip_at(r)
        lines = [[] for _ in range(vectors)]
        rights = []
        for t in range(2 * slots):
            source = xbuf[r, sector + 2 - shift_ref[chip * 2 * slots + t]]
            side = jnp.concatenate([source[v] for v in range(vectors)], axis=1)
            inner = jnp.dot(lbuf[t, k, sector], side, preferred_element_type=jnp.float32)
            inner = inner.astype(jnp.bfloat16)
            for v in range(vectors):
                lines[v].append(inner[:, v * width:(v + 1) * width])
            rights.append(rbuf[t, k, sector])
        inner = jnp.concatenate([jnp.concatenate(line, axis=1) for line in lines], axis=0)
        total = lax.dot_general(
            inner, jnp.concatenate(rights, axis=1), (((1,), (1,)), ((), ())),
            preferred_element_type=jnp.float32,
        )
        return total.reshape((vectors, width, width))

    def rs_copy(d, k):
        return pltpu.make_async_remote_copy(
            src_ref=sbuf.at[d, k], dst_ref=gbuf.at[d, k],
            send_sem=rs_send.at[d, k], recv_sem=rs_recv.at[d, k],
            device_id=nexts[d], device_id_type=MESH,
        )

    def scatter_step(k, add):
        for d in range(2):
            r = wrap(pos + signs[d] * (half_ring - (k + 1) // 2))
            h = half_of(d, k)
            if isinstance(k, int) and k == 2:
                @pl.loop(0, half)
                def _(i):
                    head_copy(d, i).wait_recv()
            elif add:
                rs_copy(d, k - 2).wait_recv()

            @pl.loop(0, half)
            def _(i):
                total = product(r, h * half + i)
                if add:
                    total = total + gbuf[d, k - 2, i].astype(jnp.float32)
                sbuf[d, k, i] = total.astype(jnp.bfloat16)

            rs_copy(d, k).start()

    def head_copy(d, i):
        return pltpu.make_async_remote_copy(
            src_ref=sbuf.at[d, 0, i], dst_ref=gbuf.at[d, 0, i],
            send_sem=head_send.at[d, i], recv_sem=head_recv.at[d, i],
            device_id=nexts[d], device_id_type=MESH,
        )

    @pl.loop(0, half, unroll=True)
    def _(i):
        for d in range(2):
            r = wrap(pos + signs[d] * half_ring)
            sbuf[d, 0, i] = product(r, d * half + i).astype(jnp.bfloat16)
            head_copy(d, i).start()

    scatter_step(1, False)
    scatter_step(2, True)

    @pl.loop(3, items)
    def _(k):
        scatter_step(k, True)

    @pl.loop(0, per)
    def _(i):
        out_ref[i] = product(pos, i)

    for k in range(items - 2, items):
        for d in range(2):
            h = k % 2 if d == 0 else 1 - k % 2
            rs_copy(d, k).wait_recv()

            @pl.loop(0, half)
            def _(i):
                value = out_ref[h * half + i] + gbuf[d, k, i].astype(jnp.float32)
                if k == items - 1:
                    live = live_ref[h * half + i]
                    down = lax.broadcasted_iota(jnp.int32, (width, width), 0)
                    along = lax.broadcasted_iota(jnp.int32, (width, width), 1)
                    keep = ((down < live) & (along < live))[None]
                    value = jnp.where(keep, value, jnp.float32(0.0))
                out_ref[h * half + i] = value

    @pl.loop(0, items)
    def _(k):
        for d in range(2):
            ag_copy(d, k, wrap(pos - signs[d] * (k // 2)), half_of(d, k)).wait_send()

    @pl.loop(1, items)
    def _(k):
        for d in range(2):
            rs_copy(d, k).wait_send()

    @pl.loop(0, half)
    def _(i):
        for d in range(2):
            head_copy(d, i).wait_send()

    @pl.loop(0, n)
    def _(r):
        for h in range(2):
            halo_copy(r, h, xbuf.at[r, 1 + h * (per - 1)]).wait_send()

    for _, remote, _ in env_copies():
        remote.wait_send()


def ring_sum(wavefunction, left_env, right_env, term_shift, sector_width):
    n = lax.axis_size("op") // 2
    slots = left_env.shape[0]
    per, vectors, width, _ = wavefunction.shape
    items = 2 * (n // 2) - 1
    shaped = (slots, n, 2, per, width, width)
    env = (2 * slots, n, per, width, width)
    dma = pltpu.SemaphoreType.DMA
    work = 2 * slots * n * per * vectors * width ** 3 * 4
    return pl.pallas_call(
        functools.partial(kernel, n, slots, per),
        out_shape=jax.ShapeDtypeStruct(wavefunction.shape, jnp.float32),
        in_specs=[
            pl.BlockSpec(memory_space=pltpu.SMEM),
            pl.BlockSpec(memory_space=pltpu.SMEM),
            pl.BlockSpec(memory_space=pltpu.HBM),
            pl.BlockSpec(memory_space=pltpu.HBM),
            pl.BlockSpec(memory_space=pltpu.HBM),
        ],
        out_specs=pl.BlockSpec(memory_space=pltpu.VMEM),
        scratch_shapes=[
            pltpu.VMEM(env, jnp.bfloat16),
            pltpu.VMEM(env, jnp.bfloat16),
            pltpu.VMEM((n, per + 2, vectors, width, width), jnp.bfloat16),
            pltpu.VMEM((2, items, per // 2, vectors, width, width), jnp.bfloat16),
            pltpu.VMEM((2, items, per // 2, vectors, width, width), jnp.bfloat16),
            dma((2, items)), dma((2, items)), dma((2, items)), dma((2, items)),
            dma((n, 2)), dma((n, 2)), dma((2,)), dma((2,)), dma((2,)), dma((1,)),
            dma((2, per // 2)), dma((2, per // 2)),
        ],
        compiler_params=pltpu.CompilerParams(
            collective_id=0, has_side_effects=True, vmem_limit_bytes=48 * 2 ** 20
        ),
        cost_estimate=pl.CostEstimate(flops=work, bytes_accessed=2 * left_env.size * 2, transcendentals=0),
    )(term_shift, sector_width, wavefunction, left_env.reshape(shaped), right_env.reshape(shaped))


def gathered_sum(wavefunction, left_env, right_env, term_shift):
    devices = lax.axis_size("op")
    split_count = max(1, devices // TERMS)
    slot_dev = left_env.shape[0]
    half_sec = left_env.shape[1]
    block_tail = wavefunction.shape[1:]
    gathered = lax.all_gather(wavefunction, "op", axis=0, tiled=True)
    zero_block = jnp.zeros((1,) + block_tail, gathered.dtype)
    padded = jnp.concatenate([zero_block, gathered, zero_block], axis=0)
    my_index = lax.axis_index("op")
    places = jnp.arange(half_sec, dtype=jnp.int32)
    partial_value = jnp.zeros((half_sec,) + block_tail, jnp.float32)
    for slot_index in range(slot_dev):
        slot_rank = my_index * slot_dev + slot_index
        half_index = slot_rank // TERMS
        term_index = slot_rank % TERMS
        shift_value = term_shift[term_index] - 1
        row_index = places * split_count + half_index - shift_value + 1
        source = jnp.take(padded, row_index, axis=0)
        inner_block = jnp.einsum(
            "qij,qvjk->qvik", left_env[slot_index], source, preferred_element_type=jnp.float32
        ).astype(jnp.bfloat16)
        partial_value = partial_value + jnp.einsum(
            "qvik,qlk->qvil", inner_block, right_env[slot_index], preferred_element_type=jnp.float32
        )
    arrived = lax.all_to_all(partial_value, "op", split_axis=0, concat_axis=0, tiled=True)
    per_peer = half_sec // devices
    grouped = arrived.reshape((split_count, devices // split_count, per_peer) + block_tail)
    summed = jnp.sum(grouped, axis=1)
    return jnp.swapaxes(summed, 0, 1).reshape(wavefunction.shape)


def per_device(wavefunction, left_env, right_env, term_shift, sector_width):
    devices = lax.axis_size("op")
    fits = devices <= TERMS and devices % 4 == 0 and devices >= 8 and wavefunction.shape[0] % 2 == 0
    if fits:
        return ring_sum(wavefunction, left_env, right_env, term_shift, sector_width)
    summed = gathered_sum(wavefunction, left_env, right_env, term_shift)
    line_index = jnp.arange(wavefunction.shape[2], dtype=jnp.int32)
    widths = sector_width[:, None, None]
    keep_mask = (line_index[None, :, None] < widths) & (line_index[None, None, :] < widths)
    return jnp.where(keep_mask[:, None], summed, jnp.float32(0.0))


def solution(mesh):
    return jax.shard_map(
        per_device,
        mesh=mesh,
        in_specs=(
            P(("groups", "op"), None, None, None),
            P(("groups", "op"), None, None, None),
            P(("groups", "op"), None, None, None),
            P("groups"),
            P(("groups", "op")),
        ),
        out_specs=P(("groups", "op"), None, None, None),
        check_vma=False,
    )
```
